32 devices in a mesh: level: 2 (over x), row: 4 (over y, core), col: 4 (over z).
Axes of the slice: x: 2, y: 2, z: 4, core: 2. Of those that a mesh axis runs over, the one named last changes fastest.
Arguments:
- initials: float32 [4096, 4, 1536], P(('level', 'row'), 'col'), may hold values from -70 to 70, as said below
- patches: int32 [2, 32], replicated, may hold values from 0 to 5
- halves: int32 [1, 32], replicated, may hold values 0 or 1
Outputs:
- panels: float32 [2, 4096, 512], P(None, ('level', 'row'), 'col')
- root_update: float32 [4096, 4, 1024], P(('level', 'row'), 'col')
The draws below stay inside these ranges and needn't reach their ends.
Inputs may be any that keep to these rules, and one draw needn't show every extreme that they name: Each front's block of initials is symmetric, and stays positive definite when multiplied by the tile mask of its level's patches.
All inputs are finite; a program needn't handle non-finite values.
Results may differ from the reference program's by a relative error of at most 0.0001.
Values sent between devices are 32-bit elements; how exact they have to be, the bound alone decides.
A program may use at most 192 MiB of HBM per device.

```python
import math
import jax
import jax.numpy as jnp
from jax import lax

TILE = 128
LEVELS = 2
TILES_ALL = 32
N_LEVEL = 2
N_ROW = 4
N_COL = 4


couple_weight = 4.0


def tile_labels(key):
    return jax.random.randint(jax.random.fold_in(key, 101), (LEVELS, TILES_ALL), 0, 6).astype(jnp.int32)


def draw_patches(key, part):
    return tile_labels(key)


def draw_initials(key, part):
    labels = tile_labels(key)
    pieces = []
    for level_k in range(LEVELS):
        group = 2 ** level_k
        order = group * N_ROW * N_COL * TILE
        fronts = N_LEVEL // group
        tiles_front = group * N_ROW * N_COL
        level_key = jax.random.fold_in(key, 17 + level_k)
        key_off, key_diag = jax.random.split(level_key, 2)
        key_low = jax.random.fold_in(level_key, 5)
        half = 1.84 / math.sqrt(order)
        raw = jax.random.uniform(key_off, (fronts, order, order), jnp.float32, -half, half)
        sym = 0.5 * (raw + jnp.swapaxes(raw, 1, 2))
        diag = jax.random.uniform(key_diag, (fronts, order), jnp.float32, 2.5, 5.0)
        ident = jnp.eye(order, dtype=bool)
        matrix = jnp.where(ident[None, :, :], diag[:, :, None], sym)
        row_labels = jnp.repeat(labels[level_k].reshape(fronts, tiles_front), TILE, axis=1)
        groups = jnp.arange(5, dtype=jnp.int32)
        member = ((groups[None, None, :] == row_labels[:, :, None] - 1) | (groups[None, None, :] == row_labels[:, :, None])).astype(jnp.float32)
        count = jnp.sum(member, axis=2, keepdims=True)
        amplitude = member * jnp.sqrt(3.0 * couple_weight / (TILE * count))
        factor = jax.random.uniform(key_low, (fronts, order, 5, TILE), jnp.float32, -1.0, 1.0) * amplitude[:, :, :, None]
        factor = factor.reshape(fronts, order, 5 * TILE)
        coupling = jnp.einsum('fxr,fyr->fxy', factor, factor, precision=lax.Precision.HIGHEST)
        matrix = matrix + 0.5 * (coupling + jnp.swapaxes(coupling, 1, 2))
        count_j = group * N_ROW
        matrix = matrix.reshape(fronts * order, count_j, N_COL, TILE).transpose(0, 2, 1, 3).reshape(fronts * order, N_COL, count_j * TILE)
        pieces.append(matrix)
    return jnp.concatenate(pieces, axis=2)


def touch_ends(result, stream_key, smallest, top_value):
    extent = result.shape
    spot = [jax.random.randint(jax.random.fold_in(stream_key, axis), (), 0, extent[axis]) for axis in range(len(extent))]
    result = result.at[tuple(spot)].set(smallest)
    longest = extent.index(max(extent))
    spot[longest] = (spot[longest] + 1) % extent[longest]
    return result.at[tuple(spot)].set(top_value)


def setup_inputs(seed: int = 0) -> dict:
    arg_keys = jax.random.split(jax.random.key(seed), 4)
    return {
        "initials": draw_initials(jax.random.fold_in(arg_keys[3], 71), 0),
        "patches": draw_patches(jax.random.fold_in(arg_keys[3], 71), 0),
        "halves": touch_ends((jax.random.randint(arg_keys[2], (LEVELS - 1, TILES_ALL), 0, 2) < 1).astype(jnp.int32), jax.random.fold_in(arg_keys[2], 1), 0, 1),
    }


def natural_order(stored, n_col, tile):
    rows_all = stored.shape[0]
    count_j = stored.shape[2] // tile
    return stored.reshape(rows_all, n_col, count_j, tile).transpose(0, 2, 1, 3).reshape(rows_all, count_j * n_col * tile)

def stored_order(matrix, n_col, tile):
    rows_all = matrix.shape[0]
    count_j = matrix.shape[1] // (n_col * tile)
    return matrix.reshape(rows_all, count_j, n_col, tile).transpose(0, 2, 1, 3).reshape(rows_all, n_col, count_j * tile)

def reference(initials, patches, halves):
    pivots = N_COL * TILE
    offset = 0
    previous = []
    panel_list = []
    for level_k in range(LEVELS):
        group = 2 ** level_k
        order = group * N_ROW * N_COL * TILE
        tiles_front = group * N_ROW * N_COL
        width = group * N_ROW * TILE
        level_block = natural_order(initials[:, :, offset:offset + width], N_COL, TILE)
        offset = offset + width
        updates = []
        panel_rows = []
        for front_q in range(N_LEVEL // group):
            front = level_block[front_q * order:(front_q + 1) * order]
            labels = patches[level_k, front_q * tiles_front:(front_q + 1) * tiles_front]
            coupled = (jnp.abs(labels[:, None] - labels[None, :]) <= 1) | jnp.eye(tiles_front, dtype=bool)
            cells = jnp.repeat(jnp.repeat(coupled.astype(jnp.float32), TILE, axis=0), TILE, axis=1)
            front = front * cells
            if level_k > 0:
                child_tiles = tiles_front // 2
                for side in range(2):
                    child = front_q * 2 + side
                    upd = previous[child]
                    hvec = halves[level_k - 1, child * child_tiles:(child + 1) * child_tiles]
                    target = jnp.arange(child_tiles) + child_tiles * hvec
                    index = (target[:, None] * TILE + jnp.arange(TILE)[None, :]).reshape(-1)
                    partial_value = jnp.zeros((order, upd.shape[1]), jnp.float32).at[index].set(upd)
                    placed = jnp.zeros((order, order), jnp.float32).at[:, index].set(partial_value)
                    front = front + placed
            factor = jnp.linalg.cholesky(front[:pivots, :pivots])
            panel = jax.scipy.linalg.solve_triangular(factor, front[:, :pivots].T, lower=True).T
            schur = front - jnp.dot(panel.astype(jnp.float32), panel.T.astype(jnp.float32), precision=lax.Precision.HIGHEST, preferred_element_type=jnp.float32)
            keep = (jnp.arange(order) >= pivots).astype(jnp.float32)
            updates.append(schur * keep[:, None] * keep[None, :])
            panel_rows.append(panel)
        panel_list.append(jnp.concatenate(panel_rows, axis=0))
        previous = updates
    root = stored_order(previous[0], N_COL, TILE)
    return (jnp.stack(panel_list, axis=0), root)
```

```python
import functools

import jax
import jax.numpy as jnp
from jax import lax
from jax.experimental import pallas as pl
from jax.experimental.pallas import tpu as pltpu
from jax.sharding import PartitionSpec as P

HIGHEST = lax.Precision.HIGHEST


def from_partner(value, axis, bit):
    mask = 2**bit
    pairs = [(source, source ^ mask) for source in range(lax.axis_size(axis))]
    return lax.ppermute(value, axis, pairs)


def pick_column(vector, start, count_j, n_col, col_idx):
    segment = lax.dynamic_slice_in_dim(vector, start, count_j * n_col).reshape(count_j, n_col)
    onehot = jnp.arange(n_col) == col_idx
    return jnp.sum(jnp.where(onehot[None, :], segment, 0), axis=1)


def place_update(update, row_half, col_half, side, tile):
    row_keep = jnp.repeat(row_half == side, tile)
    col_high = jnp.repeat(col_half == 1, tile)
    lower_part = jnp.where(row_keep[:, None] & ~col_high[None, :], update, 0.0)
    upper_part = jnp.where(row_keep[:, None] & col_high[None, :], update, 0.0)
    return jnp.concatenate([lower_part, upper_part], axis=1)


def spread_lane(value, lane):
    return jnp.broadcast_to(value[:, lane : lane + 1], value.shape)


def inverse_factor(blocks):
    n = blocks[0].shape[0]
    lane = lax.broadcasted_iota(jnp.int32, (8, n), 1)
    sub = lax.broadcasted_iota(jnp.int32, (8, n), 0)
    states = [[block[8 * v : 8 * v + 8] for v in range(n // 8)] for block in blocks]
    results = [[] for _ in blocks]
    for step in range(n // 8):
        first = 8 * step
        inside = (lane >= first) & (lane < first + 8)
        for rows, done in zip(states, results):
            head = rows[step]
            row = [jnp.broadcast_to(head[j : j + 1], (8, n)) for j in range(8)]
            small = {(i, j): spread_lane(row[j], first + i) for j in range(8) for i in range(j, 8)}
            hat = [
                jnp.where(inside, jnp.where(lane == first + j, 1.0, 0.0), row[j]) for j in range(8)
            ]
            inv = []
            mult = {}
            for j in range(8):
                inv.append(1.0 / small[j, j])
                for i in range(j + 1, 8):
                    mult[i, j] = small[i, j] * inv[j]
                for i in range(j + 1, 8):
                    for m in range(j + 1, i + 1):
                        small[i, m] = small[i, m] - mult[i, j] * small[m, j]
                    hat[i] = hat[i] - mult[i, j] * hat[j]
            own = jnp.zeros((8, n), jnp.float32)
            for j in range(8):
                pivot = small[j, j]
                root = lax.rsqrt(pivot)
                root = root * (1.5 - 0.5 * pivot * root * root)
                own = jnp.where(sub == j, hat[j] * root, own)
            done.append(jnp.where(lane <= sub + first, own, 0.0))
            back = [None] * 8
            for i in range(7, -1, -1):
                value = hat[i] * inv[i]
                for j in range(i + 1, 8):
                    value = value - mult[j, i] * back[j]
                back[i] = value
            for v in range(step + 1, n // 8):
                parts = [spread_lane(rows[v], first + i) * back[i] for i in range(8)]
                while len(parts) > 1:
                    parts = [a + b for a, b in zip(parts[::2], parts[1::2])]
                rows[v] = jnp.where(inside, 0.0, rows[v]) - parts[0]
    return [jnp.concatenate(done, axis=0) for done in results]


def invert_kernel(a_ref, out_ref):
    fronts, pivots, _ = a_ref.shape
    tile = 128
    out_ref[...] = a_ref[...]
    col = lax.broadcasted_iota(jnp.int32, (tile, pivots), 1)
    big_col = lax.broadcasted_iota(jnp.int32, (pivots, pivots), 1)
    big_row = lax.broadcasted_iota(jnp.int32, (pivots, pivots), 0)

    def body(b, carry):
        start = pl.multiple_of(b * tile, tile)
        here = pl.ds(start, tile)
        diag = inverse_factor([out_ref[f, here, here] for f in range(fronts)])
        for f in range(fronts):
            row = jnp.dot(
                diag[f], out_ref[f, here, :], precision=HIGHEST, preferred_element_type=jnp.float32
            )
            inside = (col >= start) & (col < start + tile)
            wide = jnp.concatenate([diag[f]] * (pivots // tile), axis=1)
            row = jnp.where(inside, wide, row)
            below = jnp.where(col >= start + tile, row, 0.0)
            change = lax.dot_general(
                below,
                row,
                (((0,), (0,)), ((), ())),
                precision=HIGHEST,
                preferred_element_type=jnp.float32,
            )
            clear = (big_col >= start) & (big_col < start + tile) & (big_row >= start + tile)
            out_ref[f] = jnp.where(clear, 0.0, out_ref[f]) - change
            out_ref[f, here, :] = jnp.where(col < start + tile, row, 0.0)
        return carry

    lax.fori_loop(0, pivots // tile, body, 0)


def invert(pivot_blocks):
    return pl.pallas_call(
        invert_kernel,
        out_shape=jax.ShapeDtypeStruct(pivot_blocks.shape, jnp.float32),
        in_specs=[pl.BlockSpec(memory_space=pltpu.VMEM)],
        out_specs=pl.BlockSpec(memory_space=pltpu.VMEM),
        compiler_params=pltpu.CompilerParams(vmem_limit_bytes=40 * 2**20),
        cost_estimate=pl.CostEstimate(flops=60 * 10**9, bytes_accessed=4 * 2**20, transcendentals=0),
    )(pivot_blocks)


def dot(a, b, contract):
    return lax.dot_general(
        a, b, ((contract), ((), ())), precision=HIGHEST, preferred_element_type=jnp.float32
    )


def local(initials, patches, halves):
    n_level = lax.axis_size("level")
    n_row = lax.axis_size("row")
    n_col = lax.axis_size("col")
    levels = n_level.bit_length()
    lvl = lax.axis_index("level")
    row_idx = lax.axis_index("row")
    col_idx = lax.axis_index("col")
    rows_dev = initials.shape[0]
    tile = rows_dev // n_col
    per_level = n_row * n_col
    offset = 0
    fronts = []
    for level_k in range(levels):
        group = 2**level_k
        width = group * n_row * tile
        block = initials[:, 0, offset : offset + width]
        offset = offset + width
        front_q = lvl // group
        row_tiles = per_level * lvl + n_col * row_idx + jnp.arange(n_col)
        col_tiles = front_q * per_level * group + n_col * jnp.arange(group * n_row) + col_idx
        label_rows = lax.dynamic_slice_in_dim(
            patches[level_k], per_level * lvl + n_col * row_idx, n_col
        )
        label_cols = pick_column(
            patches[level_k], front_q * per_level * group, group * n_row, n_col, col_idx
        )
        coupled = (jnp.abs(label_rows[:, None] - label_cols[None, :]) <= 1) | (
            row_tiles[:, None] == col_tiles[None, :]
        )
        cells = jnp.repeat(jnp.repeat(coupled, tile, axis=0), tile, axis=1)
        fronts.append(jnp.where(cells, block, 0.0))

    pivot_cols = jnp.stack([front[:, :tile] for front in fronts], axis=0)
    rows_piv = lax.all_gather(pivot_cols, "col", axis=2, tiled=True)
    piece = lax.dynamic_slice_in_dim(rows_piv, col_idx * tile, tile, 1)
    gathered = lax.all_gather(piece, ("level", "row"), axis=1, tiled=True)
    column_rows = []
    for level_k in range(levels):
        group = 2**level_k
        column_rows.append(
            lax.dynamic_slice_in_dim(
                gathered[level_k], lvl // group * group * n_row * tile, group * n_row * tile, 0
            )
        )
    heads = jnp.stack([rows[:tile] for rows in column_rows], axis=0)
    pivot_blocks = lax.all_gather(heads, "col", axis=1, tiled=True)
    inverses = invert(pivot_blocks)

    update = None
    panel_list = []
    for level_k in range(levels):
        group = 2**level_k
        width = group * n_row * tile
        local_level = lvl % group
        front = fronts[level_k]
        panel_rows = dot(rows_piv[level_k], inverses[level_k], ((1,), (1,)))
        panel_cols = dot(inverses[level_k], column_rows[level_k], ((1,), (1,)))
        schur = front - dot(panel_rows, panel_cols, ((1,), (0,)))
        if level_k > 0:
            child = group // 2
            side = lvl // child % 2
            partner_lvl = lvl + child - 2 * child * side
            partner_update = from_partner(update, "level", level_k - 1)
            hvec = halves[level_k - 1]
            own_rows = lax.dynamic_slice_in_dim(hvec, per_level * lvl + n_col * row_idx, n_col)
            other_rows = lax.dynamic_slice_in_dim(
                hvec, per_level * partner_lvl + n_col * row_idx, n_col
            )
            own_cols = pick_column(
                hvec, lvl // child * per_level * child, child * n_row, n_col, col_idx
            )
            other_cols = pick_column(
                hvec, partner_lvl // child * per_level * child, child * n_row, n_col, col_idx
            )
            schur = schur + place_update(update, own_rows, own_cols, side, tile)
            schur = schur + place_update(partner_update, other_rows, other_cols, side, tile)
        keep_row = ~((local_level == 0) & (row_idx == 0))
        keep_col = jnp.arange(width) >= tile
        update = jnp.where(keep_row & keep_col[None, :], schur, 0.0)
        panel_list.append(lax.dynamic_slice_in_dim(panel_rows, col_idx * tile, tile, 1))
    return (jnp.stack(panel_list, axis=0), update[:, None, :])


def solution(mesh):
    placed = (P(("level", "row"), "col", None), P(), P())
    return jax.shard_map(
        local,
        mesh=mesh,
        in_specs=placed,
        out_specs=(P(None, ("level", "row"), "col"), P(("level", "row"), "col", None)),
        check_vma=False,
    )
```

```python
import functools

import jax
import jax.numpy as jnp
from jax import lax
from jax.experimental import pallas as pl
from jax.experimental.pallas import tpu as pltpu
from jax.sharding import PartitionSpec as P

HIGHEST = lax.Precision.HIGHEST


def from_partner(value, axis, bit):
    mask = 2**bit
    pairs = [(source, source ^ mask) for source in range(lax.axis_size(axis))]
    return lax.ppermute(value, axis, pairs)


def pick_column(vector, start, count_j, n_col, col_idx):
    segment = lax.dynamic_slice_in_dim(vector, start, count_j * n_col).reshape(count_j, n_col)
    onehot = jnp.arange(n_col) == col_idx
    return jnp.sum(jnp.where(onehot[None, :], segment, 0), axis=1)


def place_update(update, row_half, col_half, side, tile):
    row_keep = jnp.repeat(row_half == side, tile)
    col_high = jnp.repeat(col_half == 1, tile)
    lower_part = jnp.where(row_keep[:, None] & ~col_high[None, :], update, 0.0)
    upper_part = jnp.where(row_keep[:, None] & col_high[None, :], update, 0.0)
    return jnp.concatenate([lower_part, upper_part], axis=1)


def spread_lane(value, lane):
    return jnp.broadcast_to(value[:, lane : lane + 1], value.shape)


def inverse_factor(blocks):
    n = blocks[0].shape[0]
    lane = lax.broadcasted_iota(jnp.int32, (8, n), 1)
    sub = lax.broadcasted_iota(jnp.int32, (8, n), 0)
    states = [[block[8 * v : 8 * v + 8] for v in range(n // 8)] for block in blocks]
    results = [[] for _ in blocks]
    for step in range(n // 8):
        first = 8 * step
        inside = (lane >= first) & (lane < first + 8)
        for rows, done in zip(states, results):
            head = rows[step]
            row = [jnp.broadcast_to(head[j : j + 1], (8, n)) for j in range(8)]
            small = {(i, j): spread_lane(row[j], first + i) for j in range(8) for i in range(j, 8)}
            hat = [
                jnp.where(inside, jnp.where(lane == first + j, 1.0, 0.0), row[j]) for j in range(8)
            ]
            inv = []
            mult = {}
            for j in range(8):
                inv.append(1.0 / small[j, j])
                for i in range(j + 1, 8):
                    mult[i, j] = small[i, j] * inv[j]
                for i in range(j + 1, 8):
                    for m in range(j + 1, i + 1):
                        small[i, m] = small[i, m] - mult[i, j] * small[m, j]
                    hat[i] = hat[i] - mult[i, j] * hat[j]
            own = jnp.zeros((8, n), jnp.float32)
            for j in range(8):
                pivot = small[j, j]
                root = lax.rsqrt(pivot)
                root = root * (1.5 - 0.5 * pivot * root * root)
                own = jnp.where(sub == j, hat[j] * root, own)
            done.append(jnp.where(lane <= sub + first, own, 0.0))
            back = [None] * 8
            for i in range(7, -1, -1):
                value = hat[i] * inv[i]
                for j in range(i + 1, 8):
                    value = value - mult[j, i] * back[j]
                back[i] = value
            for v in range(step + 1, n // 8):
                parts = [spread_lane(rows[v], first + i) * back[i] for i in range(8)]
                while len(parts) > 1:
                    parts = [a + b for a, b in zip(parts[::2], parts[1::2])]
                rows[v] = jnp.where(inside, 0.0, rows[v]) - parts[0]
    return [jnp.concatenate(done, axis=0) for done in results]


def eliminate(state, fronts, pivots, tile):
    col = lax.broadcasted_iota(jnp.int32, (tile, pivots), 1)
    big_col = lax.broadcasted_iota(jnp.int32, (pivots, pivots), 1)
    big_row = lax.broadcasted_iota(jnp.int32, (pivots, pivots), 0)

    def body(b, carry):
        start = pl.multiple_of(b * tile, tile)
        here = pl.ds(start, tile)
        diag = inverse_factor([state[f, here, here] for f in range(fronts)])
        for f in range(fronts):
            row = jnp.dot(
                diag[f], state[f, here, :], precision=HIGHEST, preferred_element_type=jnp.float32
            )
            inside = (col >= start) & (col < start + tile)
            wide = jnp.concatenate([diag[f]] * (pivots // tile), axis=1)
            row = jnp.where(inside, wide, row)
            below = jnp.where(col >= start + tile, row, 0.0)
            change = lax.dot_general(
                below,
                row,
                (((0,), (0,)), ((), ())),
                precision=HIGHEST,
                preferred_element_type=jnp.float32,
            )
            clear = (big_col >= start) & (big_col < start + tile) & (big_row >= start + tile)
            state[f] = jnp.where(clear, 0.0, state[f]) - change
            state[f, here, :] = jnp.where(col < start + tile, row, 0.0)
        return carry

    lax.fori_loop(0, pivots // tile, body, 0)


def gather_kernel(sizes, init_ref, lab_row_ref, lab_col_ref, inv_ref, rows_ref, *rest):
    n_level, n_row, n_col, levels, tile = sizes
    cols_refs = rest[:levels]
    (
        piv,
        spread_send,
        spread_recv,
        line_send,
        line_recv,
        core_send,
        core_recv,
        row_send,
        row_recv,
        col_send,
        col_recv,
        own_piv,
        own_rows,
        own_cols,
    ) = rest[levels:]
    lvl = lax.axis_index("level")
    row = lax.axis_index("row")
    col = lax.axis_index("col")
    pivots = n_col * tile
    offsets = [(2**k - 1) * n_row * tile for k in range(levels)]

    def remote(src, dst, send, recv, to):
        return pltpu.make_async_remote_copy(
            src_ref=src,
            dst_ref=dst,
            send_sem=send,
            recv_sem=recv,
            device_id=to,
            device_id_type=pl.DeviceIdType.MESH,
        )

    def tiles(index):
        return pl.ds(pl.multiple_of(index * tile, tile), tile)

    def at_col(step):
        return (lvl, row, lax.rem(col + step, n_col))

    barrier = pltpu.get_barrier_semaphore()
    greeted = 0
    for step in range(1, n_col):
        pl.semaphore_signal(
            barrier, inc=1, device_id=at_col(step), device_id_type=pl.DeviceIdType.MESH
        )
        greeted += 1
    for dl in range(n_level):
        for dr in range(n_row):
            if dl or dr:
                peer = (lax.rem(lvl + dl, n_level), lax.rem(row + dr, n_row), col)
                pl.semaphore_signal(
                    barrier, inc=1, device_id=peer, device_id_type=pl.DeviceIdType.MESH
                )
                greeted += 1
    pl.semaphore_wait(barrier, greeted)

    def row_copy(k, step, slot):
        target = lax.rem(col + step, n_col)
        which = tiles(lax.rem(target + slot, n_col))
        return remote(
            init_ref.at[which, pl.ds(offsets[k], tile)],
            rows_ref.at[k, which, tiles(col)],
            row_send.at[k, step, slot],
            row_recv.at[k, step, slot],
            at_col(step),
        )

    def row_arrival(k, step, slot):
        source = lax.rem(col + n_col - step, n_col)
        which = tiles(lax.rem(col + slot, n_col))
        return remote(
            init_ref.at[which, pl.ds(offsets[k], tile)],
            rows_ref.at[k, which, tiles(source)],
            row_send.at[k, step, slot],
            row_recv.at[k, step, slot],
            at_col(step),
        )

    def piv_tile(k, step):
        return piv.at[k, :, tiles(lax.rem(col + n_col - step, n_col))]

    def line_copy(k, step):
        return remote(
            piv_tile(k, 0), piv_tile(k, 0), line_send.at[k, step], line_recv.at[k, step], at_col(step)
        )

    def line_arrival(k, step):
        return remote(
            piv_tile(k, step),
            piv_tile(k, step),
            line_send.at[k, step],
            line_recv.at[k, step],
            at_col(step),
        )

    def core_copy(k, step):
        return remote(
            piv_tile(k, step),
            piv_tile(k, step),
            core_send.at[k, step],
            core_recv.at[k, step],
            (lvl, row // 2 * 2 + 1 - lax.rem(row, 2), col),
        )

    def spread_copy(k, slot, dl, to_row):
        return remote(
            piv_tile(k, 0),
            piv_tile(k, 0),
            spread_send.at[k, slot],
            spread_recv.at[k],
            (lax.rem(lvl + dl, n_level), to_row, col),
        )

    def col_parts(k, dl, dr, sign):
        group = 2**k
        inner = lax.rem(lvl, group)
        part_l = lax.rem(inner + (group + sign * dl), group)
        part_r = lax.rem(row + (n_row + sign * dr), n_row)
        return inner, part_l, part_r

    def col_copy(k, dl, dr):
        slot = dl * n_row + dr
        inner, to_l, to_r = col_parts(k, dl, dr, 1)
        return remote(
            rows_ref.at[k, tiles(col), :],
            cols_refs[k].at[tiles(inner * n_row + row), :],
            col_send.at[k, slot],
            col_recv.at[k, slot],
            (lvl - inner + to_l, to_r, col),
        )

    def col_arrival(k, dl, dr):
        slot = dl * n_row + dr
        inner, to_l, to_r = col_parts(k, dl, dr, 1)
        _, from_l, from_r = col_parts(k, dl, dr, -1)
        return remote(
            rows_ref.at[k, tiles(col), :],
            cols_refs[k].at[tiles(from_l * n_row + from_r), :],
            col_send.at[k, slot],
            col_recv.at[k, slot],
            (lvl - inner + to_l, to_r, col),
        )

    spread = [
        [(dl, r) for dl in range(2**k) for r in range(0, n_row, 2) if dl or r]
        for k in range(levels)
    ]
    others = [
        [(dl, dr) for dl in range(2**k) for dr in range(n_row) if dl or dr] for k in range(levels)
    ]

    def leads(k):
        return (lax.rem(lvl, 2**k) == 0) & (row == 0)

    def own_piv_copy(k):
        return pltpu.make_async_copy(
            init_ref.at[:, pl.ds(offsets[k], tile)], piv_tile(k, 0), own_piv.at[k]
        )

    def own_rows_copy(k):
        return pltpu.make_async_copy(
            init_ref.at[:, pl.ds(offsets[k], tile)], rows_ref.at[k, :, tiles(col)], own_rows.at[k]
        )

    def own_cols_copy(k):
        inner = lax.rem(lvl, 2**k)
        return pltpu.make_async_copy(
            rows_ref.at[k, tiles(col), :],
            cols_refs[k].at[tiles(inner * n_row + row), :],
            own_cols.at[k],
        )

    first_core = lax.rem(row, 2) == 0
    for k in range(levels):

        @pl.when(leads(k))
        def _(k=k):
            own_piv_copy(k).start()

    for k in range(levels):

        @pl.when(leads(k))
        def _(k=k):
            own_piv_copy(k).wait()
            for slot, (dl, r) in enumerate(spread[k]):
                spread_copy(k, slot, dl, r).start()

    for k in range(levels):
        own_rows_copy(k).start()
        for step in range(1, n_col):
            row_copy(k, step, 0).start()

    @pl.when(first_core)
    def _():
        for k in range(levels):

            @pl.when(~leads(k))
            def _(k=k):
                spread_copy(k, 0, 0, row).wait_recv()

            for step in range(1, n_col):
                line_copy(k, step).start()
            core_copy(k, 0).start()
        for k in range(levels):
            for step in range(1, n_col):
                line_arrival(k, step).wait_recv()
                core_copy(k, step).start()

    @pl.when(~first_core)
    def _():
        for k in range(levels):
            for step in range(n_col):
                core_copy(k, step).wait_recv()

    for k in range(levels):
        own_rows_copy(k).wait()
        for step in range(1, n_col):
            row_arrival(k, step, 0).wait_recv()
        own_cols_copy(k).start()
        for dl, dr in others[k]:
            col_copy(k, dl, dr).start()
    for k in range(levels):
        for slot in range(1, n_col):
            for step in range(1, n_col):
                row_copy(k, step, slot).start()

    at_row = lax.broadcasted_iota(jnp.int32, (pivots, pivots), 0) // tile
    at_column = lax.broadcasted_iota(jnp.int32, (pivots, pivots), 1) // tile
    for k in range(levels):
        near = jnp.abs(lab_row_ref[k] - lab_col_ref[k]) <= 1
        inv_ref[k] = jnp.where(near | (at_row == at_column), piv[k], 0.0)
    eliminate(inv_ref, levels, pivots, tile)

    for k in range(levels):
        own_cols_copy(k).wait()
        for step in range(1, n_col):
            row_copy(k, step, 0).wait_send()
            for slot in range(1, n_col):
                row_copy(k, step, slot).wait_send()
                row_arrival(k, step, slot).wait_recv()
        for dl, dr in others[k]:
            col_copy(k, dl, dr).wait_send()
            col_arrival(k, dl, dr).wait_recv()

        @pl.when(leads(k))
        def _(k=k):
            for slot, (dl, r) in enumerate(spread[k]):
                spread_copy(k, slot, dl, r).wait_send()

        @pl.when(first_core)
        def _(k=k):
            for step in range(n_col):
                core_copy(k, step).wait_send()
                if step:
                    line_copy(k, step).wait_send()


def gather_and_invert(initials, labels, sizes):
    n_level, n_row, n_col, levels, tile = sizes
    pivots = n_col * tile
    dma = pltpu.SemaphoreType.DMA
    square = jax.ShapeDtypeStruct((levels, pivots, pivots), jnp.float32)
    widths = [2**k * n_row * tile for k in range(levels)]
    results = pl.pallas_call(
        lambda *refs: gather_kernel(sizes, *refs),
        out_shape=[square, square]
        + [jax.ShapeDtypeStruct((width, pivots), jnp.float32) for width in widths],
        in_specs=[
            pl.BlockSpec(memory_space=pl.ANY),
            pl.BlockSpec(memory_space=pltpu.VMEM),
            pl.BlockSpec(memory_space=pltpu.VMEM),
        ],
        out_specs=[pl.BlockSpec(memory_space=pltpu.VMEM)]
        + [pl.BlockSpec(memory_space=pl.ANY)] * (levels + 1),
        scratch_shapes=[
            pltpu.VMEM((levels, pivots, pivots), jnp.float32),
            dma((levels, n_level * n_row)),
            dma((levels,)),
            dma((levels, n_col)),
            dma((levels, n_col)),
            dma((levels, n_col)),
            dma((levels, n_col)),
            dma((levels, n_col, n_col)),
            dma((levels, n_col, n_col)),
            dma((levels, n_level * n_row)),
            dma((levels, n_level * n_row)),
            dma((levels,)),
            dma((levels,)),
            dma((levels,)),
        ],
        compiler_params=pltpu.CompilerParams(
            vmem_limit_bytes=40 * 2**20, collective_id=0, has_side_effects=True
        ),
        cost_estimate=pl.CostEstimate(flops=60 * 10**9, bytes_accessed=4 * 2**20, transcendentals=0),
    )(initials, labels[:, :, None], labels[:, None, :])
    return results[0], results[1], results[2:]


def dot(a, b, contract):
    return lax.dot_general(
        a, b, ((contract), ((), ())), precision=HIGHEST, preferred_element_type=jnp.float32
    )


def local(initials, patches, halves):
    n_level = lax.axis_size("level")
    n_row = lax.axis_size("row")
    n_col = lax.axis_size("col")
    levels = n_level.bit_length()
    lvl = lax.axis_index("level")
    row_idx = lax.axis_index("row")
    col_idx = lax.axis_index("col")
    rows_dev = initials.shape[0]
    tile = rows_dev // n_col
    per_level = n_row * n_col
    sizes = (n_level, n_row, n_col, levels, tile)
    pivot_labels = jnp.stack(
        [
            lax.dynamic_slice_in_dim(patches[k], lvl // 2**k * 2**k * per_level, n_col)
            for k in range(levels)
        ]
    )
    inverses, rows_piv, column_rows = gather_and_invert(
        initials[:, 0, :], jnp.repeat(pivot_labels, tile, axis=1), sizes
    )
    offset = 0
    fronts = []
    pivot_rows = []
    pivot_columns = []
    for level_k in range(levels):
        group = 2**level_k
        width = group * n_row * tile
        block = initials[:, 0, offset : offset + width]
        offset = offset + width
        front_q = lvl // group
        first_tile = front_q * per_level * group
        row_tiles = per_level * lvl + n_col * row_idx + jnp.arange(n_col)
        col_tiles = first_tile + n_col * jnp.arange(group * n_row) + col_idx
        piv_tiles = first_tile + jnp.arange(n_col)
        label_rows = lax.dynamic_slice_in_dim(
            patches[level_k], per_level * lvl + n_col * row_idx, n_col
        )
        label_cols = pick_column(patches[level_k], first_tile, group * n_row, n_col, col_idx)

        def masked(value, labels_a, tiles_a, labels_b, tiles_b):
            coupled = (jnp.abs(labels_a[:, None] - labels_b[None, :]) <= 1) | (
                tiles_a[:, None] == tiles_b[None, :]
            )
            cells = jnp.repeat(jnp.repeat(coupled, tile, axis=0), tile, axis=1)
            return jnp.where(cells, value, 0.0)

        label_piv = pivot_labels[level_k]
        fronts.append(masked(block, label_rows, row_tiles, label_cols, col_tiles))
        pivot_rows.append(masked(rows_piv[level_k], label_rows, row_tiles, label_piv, piv_tiles))
        pivot_columns.append(
            masked(column_rows[level_k], label_cols, col_tiles, label_piv, piv_tiles)
        )

    update = None
    panel_list = []
    for level_k in range(levels):
        group = 2**level_k
        width = group * n_row * tile
        local_level = lvl % group
        front = fronts[level_k]
        panel_rows = dot(pivot_rows[level_k], inverses[level_k], ((1,), (1,)))
        panel_cols = dot(inverses[level_k], pivot_columns[level_k], ((1,), (1,)))
        schur = front - dot(panel_rows, panel_cols, ((1,), (0,)))
        if level_k > 0:
            child = group // 2
            side = lvl // child % 2
            partner_lvl = lvl + child - 2 * child * side
            partner_update = from_partner(update, "level", level_k - 1)
            hvec = halves[level_k - 1]
            own_rows = lax.dynamic_slice_in_dim(hvec, per_level * lvl + n_col * row_idx, n_col)
            other_rows = lax.dynamic_slice_in_dim(
                hvec, per_level * partner_lvl + n_col * row_idx, n_col
            )
            own_cols = pick_column(
                hvec, lvl // child * per_level * child, child * n_row, n_col, col_idx
            )
            other_cols = pick_column(
                hvec, partner_lvl // child * per_level * child, child * n_row, n_col, col_idx
            )
            schur = schur + place_update(update, own_rows, own_cols, side, tile)
            schur = schur + place_update(partner_update, other_rows, other_cols, side, tile)
        keep_row = ~((local_level == 0) & (row_idx == 0))
        keep_col = jnp.arange(width) >= tile
        update = jnp.where(keep_row & keep_col[None, :], schur, 0.0)
        panel_list.append(lax.dynamic_slice_in_dim(panel_rows, col_idx * tile, tile, 1))
    return (jnp.stack(panel_list, axis=0), update[:, None, :])


def solution(mesh):
    placed = (P(("level", "row"), "col", None), P(), P())
    return jax.shard_map(
        local,
        mesh=mesh,
        in_specs=placed,
        out_specs=(P(None, ("level", "row"), "col"), P(("level", "row"), "col", None)),
        check_vma=False,
    )
```

```python
import functools

import jax
import jax.numpy as jnp
from jax import lax
from jax.experimental import pallas as pl
from jax.experimental.pallas import tpu as pltpu
from jax.sharding import PartitionSpec as P

HIGHEST = lax.Precision.HIGHEST


def from_partner(value, axis, bit):
    mask = 2**bit
    pairs = [(source, source ^ mask) for source in range(lax.axis_size(axis))]
    return lax.ppermute(value, axis, pairs)


def pick_column(vector, start, count_j, n_col, col_idx):
    segment = lax.dynamic_slice_in_dim(vector, start, count_j * n_col).reshape(count_j, n_col)
    onehot = jnp.arange(n_col) == col_idx
    return jnp.sum(jnp.where(onehot[None, :], segment, 0), axis=1)


def place_update(update, row_half, col_half, side, tile):
    row_keep = jnp.repeat(row_half == side, tile)
    col_high = jnp.repeat(col_half == 1, tile)
    lower_part = jnp.where(row_keep[:, None] & ~col_high[None, :], update, 0.0)
    upper_part = jnp.where(row_keep[:, None] & col_high[None, :], update, 0.0)
    return jnp.concatenate([lower_part, upper_part], axis=1)


def spread_lane(value, lane):
    return jnp.broadcast_to(value[:, lane : lane + 1], value.shape)


def inverse_factor(blocks):
    n = blocks[0].shape[0]
    lane = lax.broadcasted_iota(jnp.int32, (8, n), 1)
    sub = lax.broadcasted_iota(jnp.int32, (8, n), 0)
    states = [[block[8 * v : 8 * v + 8] for v in range(n // 8)] for block in blocks]
    results = [[] for _ in blocks]
    for step in range(n // 8):
        first = 8 * step
        inside = (lane >= first) & (lane < first + 8)
        for rows, done in zip(states, results):
            head = rows[step]
            row = [jnp.broadcast_to(head[j : j + 1], (8, n)) for j in range(8)]
            small = {(i, j): spread_lane(row[j], first + i) for j in range(8) for i in range(j, 8)}
            hat = [
                jnp.where(inside, jnp.where(lane == first + j, 1.0, 0.0), row[j]) for j in range(8)
            ]
            inv = []
            mult = {}
            for j in range(8):
                inv.append(1.0 / small[j, j])
                for i in range(j + 1, 8):
                    mult[i, j] = small[i, j] * inv[j]
                for i in range(j + 1, 8):
                    for m in range(j + 1, i + 1):
                        small[i, m] = small[i, m] - mult[i, j] * small[m, j]
                    hat[i] = hat[i] - mult[i, j] * hat[j]
            own = jnp.zeros((8, n), jnp.float32)
            for j in range(8):
                pivot = small[j, j]
                root = lax.rsqrt(pivot)
                root = root * (1.5 - 0.5 * pivot * root * root)
                own = jnp.where(sub == j, hat[j] * root, own)
            done.append(jnp.where(lane <= sub + first, own, 0.0))
            back = [None] * 8
            for i in range(7, -1, -1):
                value = hat[i] * inv[i]
                for j in range(i + 1, 8):
                    value = value - mult[j, i] * back[j]
                back[i] = value
            for v in range(step + 1, n // 8):
                parts = [spread_lane(rows[v], first + i) * back[i] for i in range(8)]
                while len(parts) > 1:
                    parts = [a + b for a, b in zip(parts[::2], parts[1::2])]
                rows[v] = jnp.where(inside, 0.0, rows[v]) - parts[0]
    return [jnp.concatenate(done, axis=0) for done in results]


def eliminate(state, fronts, pivots, tile, block_row, between):
    col = lax.broadcasted_iota(jnp.int32, (tile, pivots), 1)
    big_col = lax.broadcasted_iota(jnp.int32, (pivots, pivots), 1)
    big_row = lax.broadcasted_iota(jnp.int32, (pivots, pivots), 0)

    state[...] = jnp.zeros_like(state)

    def body(b, carry):
        start = pl.multiple_of(b * tile, tile)
        here = pl.ds(start, tile)
        block_row(b)
        diag = inverse_factor([state[f, here, here] for f in range(fronts)])
        between(b)
        for f in range(fronts):
            row = jnp.dot(
                diag[f], state[f, here, :], precision=HIGHEST, preferred_element_type=jnp.float32
            )
            inside = (col >= start) & (col < start + tile)
            wide = jnp.concatenate([diag[f]] * (pivots // tile), axis=1)
            row = jnp.where(inside, wide, row)
            below = jnp.where(col >= start + tile, row, 0.0)
            change = lax.dot_general(
                below,
                row,
                (((0,), (0,)), ((), ())),
                precision=HIGHEST,
                preferred_element_type=jnp.float32,
            )
            clear = (big_col >= start) & (big_col < start + tile) & (big_row >= start + tile)
            state[f] = jnp.where(clear, 0.0, state[f]) - change
            state[f, here, :] = jnp.where(col < start + tile, row, 0.0)
        return carry

    lax.fori_loop(0, pivots // tile, body, 0)


def gather_kernel(sizes, init_ref, lab_row_ref, lab_col_ref, inv_ref, rows_ref, *rest):
    n_level, n_row, n_col, levels, tile = sizes
    cols_refs = rest[:levels]
    (
        piv,
        spread_send,
        spread_recv,
        line_send,
        line_recv,
        core_send,
        core_recv,
        row_send,
        row_recv,
        col_send,
        col_recv,
        own_piv,
        own_rows,
        own_cols,
    ) = rest[levels:]
    lvl = lax.axis_index("level")
    row = lax.axis_index("row")
    col = lax.axis_index("col")
    pivots = n_col * tile
    offsets = [(2**k - 1) * n_row * tile for k in range(levels)]

    def remote(src, dst, send, recv, to):
        return pltpu.make_async_remote_copy(
            src_ref=src,
            dst_ref=dst,
            send_sem=send,
            recv_sem=recv,
            device_id=to,
            device_id_type=pl.DeviceIdType.MESH,
        )

    def tiles(index):
        return pl.ds(pl.multiple_of(index * tile, tile), tile)

    def at_col(step):
        return (lvl, row, lax.rem(col + step, n_col))

    barrier = pltpu.get_barrier_semaphore()
    greeted = 0
    for step in range(1, n_col):
        pl.semaphore_signal(
            barrier, inc=1, device_id=at_col(step), device_id_type=pl.DeviceIdType.MESH
        )
        greeted += 1
    for dl in range(n_level):
        for dr in range(n_row):
            if dl or dr:
                peer = (lax.rem(lvl + dl, n_level), lax.rem(row + dr, n_row), col)
                pl.semaphore_signal(
                    barrier, inc=1, device_id=peer, device_id_type=pl.DeviceIdType.MESH
                )
                greeted += 1
    pl.semaphore_wait(barrier, greeted)

    def row_copy(k, step, slot):
        target = lax.rem(col + step, n_col)
        which = tiles(lax.rem(target + slot, n_col))
        return remote(
            init_ref.at[which, pl.ds(offsets[k], tile)],
            rows_ref.at[k, which, tiles(col)],
            row_send.at[k, step, slot],
            row_recv.at[k, step, slot],
            at_col(step),
        )

    def row_arrival(k, step, slot):
        source = lax.rem(col + n_col - step, n_col)
        which = tiles(lax.rem(col + slot, n_col))
        return remote(
            init_ref.at[which, pl.ds(offsets[k], tile)],
            rows_ref.at[k, which, tiles(source)],
            row_send.at[k, step, slot],
            row_recv.at[k, step, slot],
            at_col(step),
        )

    def piv_tile(k, step, r):
        return piv.at[k, tiles(r), tiles(lax.rem(col + n_col - step, n_col))]

    def line_copy(k, step, r):
        return remote(
            piv_tile(k, 0, r),
            piv_tile(k, 0, r),
            line_send.at[k, step, r],
            line_recv.at[k, step, r],
            at_col(step),
        )

    def line_arrival(k, step, r):
        return remote(
            piv_tile(k, step, r),
            piv_tile(k, step, r),
            line_send.at[k, step, r],
            line_recv.at[k, step, r],
            at_col(step),
        )

    def core_copy(k, step, r):
        return remote(
            piv_tile(k, step, r),
            piv_tile(k, step, r),
            core_send.at[k, step, r],
            core_recv.at[k, step, r],
            (lvl, row // 2 * 2 + 1 - lax.rem(row, 2), col),
        )

    def spread_copy(k, slot, dl, to_row, r):
        return remote(
            piv_tile(k, 0, r),
            piv_tile(k, 0, r),
            spread_send.at[k, slot, r],
            spread_recv.at[k, r],
            (lax.rem(lvl + dl, n_level), to_row, col),
        )

    def col_parts(k, dl, dr, sign):
        group = 2**k
        inner = lax.rem(lvl, group)
        part_l = lax.rem(inner + (group + sign * dl), group)
        part_r = lax.rem(row + (n_row + sign * dr), n_row)
        return inner, part_l, part_r

    def col_copy(k, dl, dr):
        slot = dl * n_row + dr
        inner, to_l, to_r = col_parts(k, dl, dr, 1)
        return remote(
            rows_ref.at[k, tiles(col), :],
            cols_refs[k].at[tiles(inner * n_row + row), :],
            col_send.at[k, slot],
            col_recv.at[k, slot],
            (lvl - inner + to_l, to_r, col),
        )

    def col_arrival(k, dl, dr):
        slot = dl * n_row + dr
        inner, to_l, to_r = col_parts(k, dl, dr, 1)
        _, from_l, from_r = col_parts(k, dl, dr, -1)
        return remote(
            rows_ref.at[k, tiles(col), :],
            cols_refs[k].at[tiles(from_l * n_row + from_r), :],
            col_send.at[k, slot],
            col_recv.at[k, slot],
            (lvl - inner + to_l, to_r, col),
        )

    spread = [
        [(dl, r) for dl in range(2**k) for r in range(0, n_row, 2) if dl or r]
        for k in range(levels)
    ]
    others = [
        [(dl, dr) for dl in range(2**k) for dr in range(n_row) if dl or dr] for k in range(levels)
    ]

    def leads(k):
        return (lax.rem(lvl, 2**k) == 0) & (row == 0)

    def own_piv_copy(k):
        return pltpu.make_async_copy(
            init_ref.at[:, pl.ds(offsets[k], tile)], piv.at[k, :, tiles(col)], own_piv.at[k]
        )

    def own_rows_copy(k):
        return pltpu.make_async_copy(
            init_ref.at[:, pl.ds(offsets[k], tile)], rows_ref.at[k, :, tiles(col)], own_rows.at[k]
        )

    def own_cols_copy(k):
        inner = lax.rem(lvl, 2**k)
        return pltpu.make_async_copy(
            rows_ref.at[k, tiles(col), :],
            cols_refs[k].at[tiles(inner * n_row + row), :],
            own_cols.at[k],
        )

    first_core = lax.rem(row, 2) == 0
    for k in range(levels):

        @pl.when(leads(k))
        def _(k=k):
            own_piv_copy(k).start()

    for k in range(levels):

        @pl.when(leads(k))
        def _(k=k):
            own_piv_copy(k).wait()

    for r in range(n_col):
        for k in range(levels):

            @pl.when(leads(k))
            def _(k=k, r=r):
                for slot, (dl, to_row) in enumerate(spread[k]):
                    spread_copy(k, slot, dl, to_row, r).start()

    for k in range(levels):
        own_rows_copy(k).start()

    @pl.when(first_core)
    def _():
        for r in range(n_col):
            for k in range(levels):

                @pl.when(~leads(k))
                def _(k=k, r=r):
                    spread_copy(k, 0, 0, row, r).wait_recv()

                for step in range(1, n_col):
                    line_copy(k, step, r).start()
                core_copy(k, 0, r).start()

    for k in range(levels):
        for step in range(1, n_col):
            row_copy(k, step, 0).start()

    def advance(r):
        @pl.when(first_core)
        def _():
            for k in range(levels):
                for step in range(1, n_col):
                    line_arrival(k, step, r).wait_recv()
                    core_copy(k, step, r).start()

    wide_col = lax.broadcasted_iota(jnp.int32, (tile, pivots), 1)

    def block_row(b):
        @pl.when(~first_core)
        def _():
            for k in range(levels):
                for step in range(n_col):
                    core_copy(k, step, b).wait_recv()

        here = tiles(b)
        start = b * tile
        for k in range(levels):
            near = jnp.abs(lab_row_ref[k, here, :] - lab_col_ref[k]) <= 1
            same = wide_col < start + tile
            keep = (near | same) & (wide_col >= start)
            inv_ref[k, here, :] = inv_ref[k, here, :] + jnp.where(keep, piv[k, here, :], 0.0)

    def between(b):
        @pl.when(b < n_col - 1)
        def _():
            advance(b + 1)

        @pl.when(b == 0)
        def _():
            for k in range(levels):
                own_rows_copy(k).wait()
                for step in range(1, n_col):
                    row_arrival(k, step, 0).wait_recv()
                own_cols_copy(k).start()
                for dl, dr in others[k]:
                    col_copy(k, dl, dr).start()
            for k in range(levels):
                for slot in range(1, n_col):
                    for step in range(1, n_col):
                        row_copy(k, step, slot).start()

    advance(0)
    eliminate(inv_ref, levels, pivots, tile, block_row, between)

    for k in range(levels):
        own_cols_copy(k).wait()
        for step in range(1, n_col):
            row_copy(k, step, 0).wait_send()
            for slot in range(1, n_col):
                row_copy(k, step, slot).wait_send()
                row_arrival(k, step, slot).wait_recv()
        for dl, dr in others[k]:
            col_copy(k, dl, dr).wait_send()
            col_arrival(k, dl, dr).wait_recv()

        @pl.when(leads(k))
        def _(k=k):
            for slot, (dl, to_row) in enumerate(spread[k]):
                for r in range(n_col):
                    spread_copy(k, slot, dl, to_row, r).wait_send()

        @pl.when(first_core)
        def _(k=k):
            for step in range(n_col):
                for r in range(n_col):
                    core_copy(k, step, r).wait_send()
                    if step:
                        line_copy(k, step, r).wait_send()


def gather_and_invert(initials, labels, sizes):
    n_level, n_row, n_col, levels, tile = sizes
    pivots = n_col * tile
    dma = pltpu.SemaphoreType.DMA
    square = jax.ShapeDtypeStruct((levels, pivots, pivots), jnp.float32)
    widths = [2**k * n_row * tile for k in range(levels)]
    results = pl.pallas_call(
        lambda *refs: gather_kernel(sizes, *refs),
        out_shape=[square, square]
        + [jax.ShapeDtypeStruct((width, pivots), jnp.float32) for width in widths],
        in_specs=[
            pl.BlockSpec(memory_space=pl.ANY),
            pl.BlockSpec(memory_space=pltpu.VMEM),
            pl.BlockSpec(memory_space=pltpu.VMEM),
        ],
        out_specs=[pl.BlockSpec(memory_space=pltpu.VMEM)]
        + [pl.BlockSpec(memory_space=pl.ANY)] * (levels + 1),
        scratch_shapes=[
            pltpu.VMEM((levels, pivots, pivots), jnp.float32),
            dma((levels, n_level * n_row, n_col)),
            dma((levels, n_col)),
            dma((levels, n_col, n_col)),
            dma((levels, n_col, n_col)),
            dma((levels, n_col, n_col)),
            dma((levels, n_col, n_col)),
            dma((levels, n_col, n_col)),
            dma((levels, n_col, n_col)),
            dma((levels, n_level * n_row)),
            dma((levels, n_level * n_row)),
            dma((levels,)),
            dma((levels,)),
            dma((levels,)),
        ],
        compiler_params=pltpu.CompilerParams(
            vmem_limit_bytes=40 * 2**20, collective_id=0, has_side_effects=True
        ),
        cost_estimate=pl.CostEstimate(flops=60 * 10**9, bytes_accessed=4 * 2**20, transcendentals=0),
    )(initials, labels[:, :, None], labels[:, None, :])
    return results[0], results[1], results[2:]


def schur_kernel(k, sizes, patches_ref, inv_ref, rows_ref, cols_ref, front_ref, panel_ref, out_ref, panel):
    n_row, n_col, tile = sizes
    group = 2**k
    j = pl.program_id(0)
    lvl = lax.axis_index("level")
    row = lax.axis_index("row")
    col = lax.axis_index("col")
    per_level = n_row * n_col
    first = lvl // group * group * per_level
    row_tiles = [per_level * lvl + n_col * row + t for t in range(n_col)]
    col_tiles = [first + n_col * (j * n_row + t) + col for t in range(n_row)]
    piv_tiles = [first + t for t in range(n_col)]

    def masked(ref, tiles_a, tiles_b):
        labels_a = [patches_ref[k, t] for t in tiles_a]
        labels_b = [patches_ref[k, t] for t in tiles_b]
        strips = []
        for a, tile_a in enumerate(tiles_a):
            parts = []
            for b, tile_b in enumerate(tiles_b):
                keep = (jnp.abs(labels_a[a] - labels_b[b]) <= 1) | (tile_a == tile_b)
                block = ref[a * tile : (a + 1) * tile, b * tile : (b + 1) * tile]
                parts.append(jnp.where(keep, block, 0.0))
            strips.append(jnp.concatenate(parts, axis=1))
        return jnp.concatenate(strips, axis=0)

    @pl.when(j == 0)
    def _():
        panel[...] = dot(masked(rows_ref, row_tiles, piv_tiles), inv_ref[...], ((1,), (1,)))
        panel_ref[...] = panel[:, pl.ds(pl.multiple_of(col * tile, tile), tile)]

    across = dot(inv_ref[...], masked(cols_ref, col_tiles, piv_tiles), ((1,), (1,)))
    schur = masked(front_ref, row_tiles, col_tiles) - dot(panel[...], across, ((1,), (0,)))
    at_col = lax.broadcasted_iota(jnp.int32, schur.shape, 1)
    lead = (lax.rem(lvl, group) == 0) & (row == 0)
    drop = (at_col < jnp.where(j == 0, tile, 0)) | (at_col < jnp.where(lead, n_row * tile, 0))
    out_ref[...] = jnp.where(drop, 0.0, schur)


def panel_and_schur(k, sizes, patches, inverses, rows_piv, columns, flat):
    n_row, n_col, tile = sizes
    group = 2**k
    high = n_col * tile
    wide = n_row * tile
    return pl.pallas_call(
        lambda *refs: schur_kernel(k, sizes, *refs),
        grid=(group,),
        out_shape=[
            jax.ShapeDtypeStruct((high, tile), jnp.float32),
            jax.ShapeDtypeStruct((high, group * wide), jnp.float32),
        ],
        in_specs=[
            pl.BlockSpec(memory_space=pltpu.SMEM),
            pl.BlockSpec((None, high, high), lambda j: (k, 0, 0)),
            pl.BlockSpec((None, high, high), lambda j: (k, 0, 0)),
            pl.BlockSpec((wide, high), lambda j: (j, 0)),
            pl.BlockSpec((high, wide), lambda j: (0, group - 1 + j)),
        ],
        out_specs=[
            pl.BlockSpec((high, tile), lambda j: (0, 0)),
            pl.BlockSpec((high, wide), lambda j: (0, j)),
        ],
        scratch_shapes=[pltpu.VMEM((high, high), jnp.float32)],
        compiler_params=pltpu.CompilerParams(vmem_limit_bytes=40 * 2**20),
        cost_estimate=pl.CostEstimate(
            flops=12 * (2 * group + 1) * high**3,
            bytes_accessed=4 * (3 * group + 2) * high * high,
            transcendentals=0,
        ),
    )(patches, inverses, rows_piv, columns, flat)


def dot(a, b, contract):
    return lax.dot_general(
        a, b, ((contract), ((), ())), precision=HIGHEST, preferred_element_type=jnp.float32
    )


def local(initials, patches, halves):
    n_level = lax.axis_size("level")
    n_row = lax.axis_size("row")
    n_col = lax.axis_size("col")
    levels = n_level.bit_length()
    lvl = lax.axis_index("level")
    row_idx = lax.axis_index("row")
    col_idx = lax.axis_index("col")
    rows_dev = initials.shape[0]
    tile = rows_dev // n_col
    per_level = n_row * n_col
    sizes = (n_level, n_row, n_col, levels, tile)
    pivot_labels = jnp.stack(
        [
            lax.dynamic_slice_in_dim(patches[k], lvl // 2**k * 2**k * per_level, n_col)
            for k in range(levels)
        ]
    )
    flat = initials[:, 0, :]
    inverses, rows_piv, column_rows = gather_and_invert(
        flat, jnp.repeat(pivot_labels, tile, axis=1), sizes
    )
    update = None
    panel_list = []
    for level_k in range(levels):
        group = 2**level_k
        width = group * n_row * tile
        local_level = lvl % group
        panel, schur = panel_and_schur(
            level_k,
            (n_row, n_col, tile),
            patches,
            inverses,
            rows_piv,
            column_rows[level_k],
            flat,
        )
        if level_k > 0:
            child = group // 2
            side = lvl // child % 2
            partner_lvl = lvl + child - 2 * child * side
            partner_update = from_partner(update, "level", level_k - 1)
            hvec = halves[level_k - 1]
            own_rows = lax.dynamic_slice_in_dim(hvec, per_level * lvl + n_col * row_idx, n_col)
            other_rows = lax.dynamic_slice_in_dim(
                hvec, per_level * partner_lvl + n_col * row_idx, n_col
            )
            own_cols = pick_column(
                hvec, lvl // child * per_level * child, child * n_row, n_col, col_idx
            )
            other_cols = pick_column(
                hvec, partner_lvl // child * per_level * child, child * n_row, n_col, col_idx
            )
            schur = schur + place_update(update, own_rows, own_cols, side, tile)
            schur = schur + place_update(partner_update, other_rows, other_cols, side, tile)
            keep_row = ~((local_level == 0) & (row_idx == 0))
            keep_col = jnp.arange(width) >= tile
            schur = jnp.where(keep_row & keep_col[None, :], schur, 0.0)
        update = schur
        panel_list.append(panel)
    return (jnp.stack(panel_list, axis=0), update[:, None, :])


def solution(mesh):
    placed = (P(("level", "row"), "col", None), P(), P())
    return jax.shard_map(
        local,
        mesh=mesh,
        in_specs=placed,
        out_specs=(P(None, ("level", "row"), "col"), P(("level", "row"), "col", None)),
        check_vma=False,
    )
```

```python
import functools

import jax
import jax.numpy as jnp
from jax import lax
from jax.experimental import pallas as pl
from jax.experimental.pallas import tpu as pltpu
from jax.sharding import PartitionSpec as P

HIGHEST = lax.Precision.HIGHEST


def from_partner(value, axis, bit):
    mask = 2**bit
    pairs = [(source, source ^ mask) for source in range(lax.axis_size(axis))]
    return lax.ppermute(value, axis, pairs)


def pick_column(vector, start, count_j, n_col, col_idx):
    segment = lax.dynamic_slice_in_dim(vector, start, count_j * n_col).reshape(count_j, n_col)
    onehot = jnp.arange(n_col) == col_idx
    return jnp.sum(jnp.where(onehot[None, :], segment, 0), axis=1)


def place_update(update, row_half, col_half, side, tile):
    row_keep = jnp.repeat(row_half == side, tile)
    col_high = jnp.repeat(col_half == 1, tile)
    lower_part = jnp.where(row_keep[:, None] & ~col_high[None, :], update, 0.0)
    upper_part = jnp.where(row_keep[:, None] & col_high[None, :], update, 0.0)
    return jnp.concatenate([lower_part, upper_part], axis=1)


def spread_lane(value, lane):
    return jnp.broadcast_to(value[:, lane : lane + 1], value.shape)


def inverse_factor(blocks):
    n = blocks[0].shape[0]
    lane = lax.broadcasted_iota(jnp.int32, (8, n), 1)
    sub = lax.broadcasted_iota(jnp.int32, (8, n), 0)
    states = [[block[8 * v : 8 * v + 8] for v in range(n // 8)] for block in blocks]
    results = [[] for _ in blocks]
    for step in range(n // 8):
        first = 8 * step
        inside = (lane >= first) & (lane < first + 8)
        for rows, done in zip(states, results):
            head = rows[step]
            row = [jnp.broadcast_to(head[j : j + 1], (8, n)) for j in range(8)]
            small = {(i, j): spread_lane(row[j], first + i) for j in range(8) for i in range(j, 8)}
            hat = [
                jnp.where(inside, jnp.where(lane == first + j, 1.0, 0.0), row[j]) for j in range(8)
            ]
            inv = []
            mult = {}
            for j in range(8):
                inv.append(1.0 / small[j, j])
                for i in range(j + 1, 8):
                    mult[i, j] = small[i, j] * inv[j]
                for i in range(j + 1, 8):
                    for m in range(j + 1, i + 1):
                        small[i, m] = small[i, m] - mult[i, j] * small[m, j]
                    hat[i] = hat[i] - mult[i, j] * hat[j]
            own = jnp.zeros((8, n), jnp.float32)
            for j in range(8):
                pivot = small[j, j]
                root = lax.rsqrt(pivot)
                root = root * (1.5 - 0.5 * pivot * root * root)
                own = jnp.where(sub == j, hat[j] * root, own)
            done.append(jnp.where(lane <= sub + first, own, 0.0))
            back = [None] * 8
            for i in range(7, -1, -1):
                value = hat[i] * inv[i]
                for j in range(i + 1, 8):
                    value = value - mult[j, i] * back[j]
                back[i] = value
            for v in range(step + 1, n // 8):
                parts = [spread_lane(rows[v], first + i) * back[i] for i in range(8)]
                while len(parts) > 1:
                    parts = [a + b for a, b in zip(parts[::2], parts[1::2])]
                rows[v] = jnp.where(inside, 0.0, rows[v]) - parts[0]
    return [jnp.concatenate(done, axis=0) for done in results]


def eliminate(state, fronts, pivots, tile, block_row, between):
    col = lax.broadcasted_iota(jnp.int32, (tile, pivots), 1)
    big_col = lax.broadcasted_iota(jnp.int32, (pivots, pivots), 1)
    big_row = lax.broadcasted_iota(jnp.int32, (pivots, pivots), 0)

    state[...] = jnp.zeros_like(state)

    def body(b, carry):
        start = pl.multiple_of(b * tile, tile)
        here = pl.ds(start, tile)
        block_row(b)
        diag = inverse_factor([state[f, here, here] for f in range(fronts)])
        between(b)
        for f in range(fronts):
            row = jnp.dot(
                diag[f], state[f, here, :], precision=HIGHEST, preferred_element_type=jnp.float32
            )
            inside = (col >= start) & (col < start + tile)
            wide = jnp.concatenate([diag[f]] * (pivots // tile), axis=1)
            row = jnp.where(inside, wide, row)
            below = jnp.where(col >= start + tile, row, 0.0)
            change = lax.dot_general(
                below,
                row,
                (((0,), (0,)), ((), ())),
                precision=HIGHEST,
                preferred_element_type=jnp.float32,
            )
            clear = (big_col >= start) & (big_col < start + tile) & (big_row >= start + tile)
            state[f] = jnp.where(clear, 0.0, state[f]) - change
            state[f, here, :] = jnp.where(col < start + tile, row, 0.0)
        return carry

    lax.fori_loop(0, pivots // tile, body, 0)


def gather_kernel(sizes, init_ref, lab_row_ref, lab_col_ref, inv_ref, rows_ref, *rest):
    n_level, n_row, n_col, levels, tile = sizes
    cols_refs = rest[:levels]
    (
        piv,
        spread_send,
        spread_recv,
        line_send,
        line_recv,
        core_send,
        core_recv,
        row_send,
        row_recv,
        col_send,
        col_recv,
        own_piv,
        own_rows,
        own_cols,
    ) = rest[levels:]
    lvl = lax.axis_index("level")
    row = lax.axis_index("row")
    col = lax.axis_index("col")
    pivots = n_col * tile
    offsets = [(2**k - 1) * n_row * tile for k in range(levels)]

    def remote(src, dst, send, recv, to):
        return pltpu.make_async_remote_copy(
            src_ref=src,
            dst_ref=dst,
            send_sem=send,
            recv_sem=recv,
            device_id=to,
            device_id_type=pl.DeviceIdType.MESH,
        )

    def tiles(index):
        return pl.ds(pl.multiple_of(index * tile, tile), tile)

    def at_col(step):
        return (lvl, row, lax.rem(col + step, n_col))

    barrier = pltpu.get_barrier_semaphore()
    greeted = 0
    for step in range(1, n_col):
        pl.semaphore_signal(
            barrier, inc=1, device_id=at_col(step), device_id_type=pl.DeviceIdType.MESH
        )
        greeted += 1
    for dl in range(n_level):
        for dr in range(n_row):
            if dl or dr:
                peer = (lax.rem(lvl + dl, n_level), lax.rem(row + dr, n_row), col)
                pl.semaphore_signal(
                    barrier, inc=1, device_id=peer, device_id_type=pl.DeviceIdType.MESH
                )
                greeted += 1
    pl.semaphore_wait(barrier, greeted)

    def row_copy(k, step, slot):
        target = lax.rem(col + step, n_col)
        which = tiles(lax.rem(target + slot, n_col))
        return remote(
            init_ref.at[which, pl.ds(offsets[k], tile)],
            rows_ref.at[k, which, tiles(col)],
            row_send.at[k, step, slot],
            row_recv.at[k, step, slot],
            at_col(step),
        )

    def row_arrival(k, step, slot):
        source = lax.rem(col + n_col - step, n_col)
        which = tiles(lax.rem(col + slot, n_col))
        return remote(
            init_ref.at[which, pl.ds(offsets[k], tile)],
            rows_ref.at[k, which, tiles(source)],
            row_send.at[k, step, slot],
            row_recv.at[k, step, slot],
            at_col(step),
        )

    def piv_tile(k, step, r):
        return piv.at[k, tiles(r), tiles(lax.rem(col + n_col - step, n_col))]

    def line_copy(k, step, r):
        return remote(
            piv_tile(k, 0, r),
            piv_tile(k, 0, r),
            line_send.at[k, step, r],
            line_recv.at[k, step, r],
            at_col(step),
        )

    def line_arrival(k, step, r):
        return remote(
            piv_tile(k, step, r),
            piv_tile(k, step, r),
            line_send.at[k, step, r],
            line_recv.at[k, step, r],
            at_col(step),
        )

    def core_copy(k, step, r):
        return remote(
            piv_tile(k, step, r),
            piv_tile(k, step, r),
            core_send.at[k, step, r],
            core_recv.at[k, step, r],
            (lvl, row // 2 * 2 + 1 - lax.rem(row, 2), col),
        )

    def spread_copy(k, slot, dl, to_row, r):
        return remote(
            piv_tile(k, 0, r),
            piv_tile(k, 0, r),
            spread_send.at[k, slot, r],
            spread_recv.at[k, r],
            (lax.rem(lvl + dl, n_level), to_row, col),
        )

    def col_parts(k, dl, dr, sign):
        group = 2**k
        inner = lax.rem(lvl, group)
        part_l = lax.rem(inner + (group + sign * dl), group)
        part_r = lax.rem(row + (n_row + sign * dr), n_row)
        return inner, part_l, part_r

    def col_copy(k, dl, dr):
        slot = dl * n_row + dr
        inner, to_l, to_r = col_parts(k, dl, dr, 1)
        return remote(
            rows_ref.at[k, tiles(col), :],
            cols_refs[k].at[tiles(inner * n_row + row), :],
            col_send.at[k, slot],
            col_recv.at[k, slot],
            (lvl - inner + to_l, to_r, col),
        )

    def col_arrival(k, dl, dr):
        slot = dl * n_row + dr
        inner, to_l, to_r = col_parts(k, dl, dr, 1)
        _, from_l, from_r = col_parts(k, dl, dr, -1)
        return remote(
            rows_ref.at[k, tiles(col), :],
            cols_refs[k].at[tiles(from_l * n_row + from_r), :],
            col_send.at[k, slot],
            col_recv.at[k, slot],
            (lvl - inner + to_l, to_r, col),
        )

    spread = [
        [(dl, r) for dl in range(2**k) for r in range(0, n_row, 2) if dl or r]
        for k in range(levels)
    ]
    others = [
        [(dl, dr) for dl in range(2**k) for dr in range(n_row) if dl or dr] for k in range(levels)
    ]

    def leads(k):
        return (lax.rem(lvl, 2**k) == 0) & (row == 0)

    def own_piv_copy(k):
        return pltpu.make_async_copy(
            init_ref.at[:, pl.ds(offsets[k], tile)], piv.at[k, :, tiles(col)], own_piv.at[k]
        )

    def own_rows_copy(k):
        return pltpu.make_async_copy(
            init_ref.at[:, pl.ds(offsets[k], tile)], rows_ref.at[k, :, tiles(col)], own_rows.at[k]
        )

    def own_cols_copy(k):
        inner = lax.rem(lvl, 2**k)
        return pltpu.make_async_copy(
            rows_ref.at[k, tiles(col), :],
            cols_refs[k].at[tiles(inner * n_row + row), :],
            own_cols.at[k],
        )

    first_core = lax.rem(row, 2) == 0
    for k in range(levels):

        @pl.when(leads(k))
        def _(k=k):
            own_piv_copy(k).start()

    for k in range(levels):

        @pl.when(leads(k))
        def _(k=k):
            own_piv_copy(k).wait()

    for r in range(n_col):
        for k in range(levels):

            @pl.when(leads(k))
            def _(k=k, r=r):
                for slot, (dl, to_row) in enumerate(spread[k]):
                    spread_copy(k, slot, dl, to_row, r).start()

    for k in range(levels):
        own_rows_copy(k).start()

    @pl.when(first_core)
    def _():
        for r in range(n_col):
            for k in range(levels):

                @pl.when(~leads(k))
                def _(k=k, r=r):
                    spread_copy(k, 0, 0, row, r).wait_recv()

                for step in range(1, n_col):
                    line_copy(k, step, r).start()
                core_copy(k, 0, r).start()

    for k in range(levels):
        for step in range(1, n_col):
            row_copy(k, step, 0).start()

    def advance(r):
        @pl.when(first_core)
        def _():
            for k in range(levels):
                for step in range(1, n_col):
                    line_arrival(k, step, r).wait_recv()
                    core_copy(k, step, r).start()

    wide_col = lax.broadcasted_iota(jnp.int32, (tile, pivots), 1)

    def block_row(b):
        @pl.when(~first_core)
        def _():
            for k in range(levels):
                for step in range(n_col):
                    core_copy(k, step, b).wait_recv()

        here = tiles(b)
        start = b * tile
        for k in range(levels):
            near = jnp.abs(lab_row_ref[k, here, :] - lab_col_ref[k]) <= 1
            same = wide_col < start + tile
            keep = (near | same) & (wide_col >= start)
            inv_ref[k, here, :] = inv_ref[k, here, :] + jnp.where(keep, piv[k, here, :], 0.0)

    def between(b):
        @pl.when(b < n_col - 1)
        def _():
            advance(b + 1)

        @pl.when(b == 0)
        def _():
            for k in range(levels):
                own_rows_copy(k).wait()
                for step in range(1, n_col):
                    row_arrival(k, step, 0).wait_recv()
                own_cols_copy(k).start()
                for dl, dr in others[k]:
                    col_copy(k, dl, dr).start()

    advance(0)
    for k in range(levels):
        for slot in range(1, n_col):
            for step in range(1, n_col):
                row_copy(k, step, slot).start()
    eliminate(inv_ref, levels, pivots, tile, block_row, between)

    for k in range(levels):
        own_cols_copy(k).wait()
        for step in range(1, n_col):
            row_copy(k, step, 0).wait_send()
            for slot in range(1, n_col):
                row_copy(k, step, slot).wait_send()
                row_arrival(k, step, slot).wait_recv()
        for dl, dr in others[k]:
            col_copy(k, dl, dr).wait_send()
            col_arrival(k, dl, dr).wait_recv()

        @pl.when(leads(k))
        def _(k=k):
            for slot, (dl, to_row) in enumerate(spread[k]):
                for r in range(n_col):
                    spread_copy(k, slot, dl, to_row, r).wait_send()

        @pl.when(first_core)
        def _(k=k):
            for step in range(n_col):
                for r in range(n_col):
                    core_copy(k, step, r).wait_send()
                    if step:
                        line_copy(k, step, r).wait_send()


def gather_and_invert(initials, labels, sizes):
    n_level, n_row, n_col, levels, tile = sizes
    pivots = n_col * tile
    dma = pltpu.SemaphoreType.DMA
    square = jax.ShapeDtypeStruct((levels, pivots, pivots), jnp.float32)
    widths = [2**k * n_row * tile for k in range(levels)]
    results = pl.pallas_call(
        lambda *refs: gather_kernel(sizes, *refs),
        out_shape=[square, square]
        + [jax.ShapeDtypeStruct((width, pivots), jnp.float32) for width in widths],
        in_specs=[
            pl.BlockSpec(memory_space=pl.ANY),
            pl.BlockSpec(memory_space=pltpu.VMEM),
            pl.BlockSpec(memory_space=pltpu.VMEM),
        ],
        out_specs=[pl.BlockSpec(memory_space=pltpu.VMEM)]
        + [pl.BlockSpec(memory_space=pl.ANY)] * (levels + 1),
        scratch_shapes=[
            pltpu.VMEM((levels, pivots, pivots), jnp.float32),
            dma((levels, n_level * n_row, n_col)),
            dma((levels, n_col)),
            dma((levels, n_col, n_col)),
            dma((levels, n_col, n_col)),
            dma((levels, n_col, n_col)),
            dma((levels, n_col, n_col)),
            dma((levels, n_col, n_col)),
            dma((levels, n_col, n_col)),
            dma((levels, n_level * n_row)),
            dma((levels, n_level * n_row)),
            dma((levels,)),
            dma((levels,)),
            dma((levels,)),
        ],
        compiler_params=pltpu.CompilerParams(
            vmem_limit_bytes=40 * 2**20, collective_id=0, has_side_effects=True
        ),
        cost_estimate=pl.CostEstimate(flops=60 * 10**9, bytes_accessed=4 * 2**20, transcendentals=0),
    )(initials, labels[:, :, None], labels[:, None, :])
    return results[0], results[1], results[2:]


def schur_kernel(k, sizes, patches_ref, inv_ref, rows_ref, cols_ref, front_ref, panel_ref, out_ref, panel):
    n_row, n_col, tile = sizes
    group = 2**k
    j = pl.program_id(0)
    lvl = lax.axis_index("level")
    row = lax.axis_index("row")
    col = lax.axis_index("col")
    per_level = n_row * n_col
    first = lvl // group * group * per_level
    row_tiles = [per_level * lvl + n_col * row + t for t in range(n_col)]
    col_tiles = [first + n_col * (j * n_row + t) + col for t in range(n_row)]
    piv_tiles = [first + t for t in range(n_col)]

    def masked(ref, tiles_a, tiles_b):
        labels_a = [patches_ref[k, t] for t in tiles_a]
        labels_b = [patches_ref[k, t] for t in tiles_b]
        strips = []
        for a, tile_a in enumerate(tiles_a):
            parts = []
            for b, tile_b in enumerate(tiles_b):
                keep = (jnp.abs(labels_a[a] - labels_b[b]) <= 1) | (tile_a == tile_b)
                block = ref[a * tile : (a + 1) * tile, b * tile : (b + 1) * tile]
                parts.append(jnp.where(keep, block, 0.0))
            strips.append(jnp.concatenate(parts, axis=1))
        return jnp.concatenate(strips, axis=0)

    @pl.when(j == 0)
    def _():
        panel[...] = dot(masked(rows_ref, row_tiles, piv_tiles), inv_ref[...], ((1,), (1,)))
        panel_ref[...] = panel[:, pl.ds(pl.multiple_of(col * tile, tile), tile)]

    across = dot(inv_ref[...], masked(cols_ref, col_tiles, piv_tiles), ((1,), (1,)))
    schur = masked(front_ref, row_tiles, col_tiles) - dot(panel[...], across, ((1,), (0,)))
    at_col = lax.broadcasted_iota(jnp.int32, schur.shape, 1)
    lead = (lax.rem(lvl, group) == 0) & (row == 0)
    drop = (at_col < jnp.where(j == 0, tile, 0)) | (at_col < jnp.where(lead, n_row * tile, 0))
    out_ref[...] = jnp.where(drop, 0.0, schur)


def panel_and_schur(k, sizes, patches, inverses, rows_piv, columns, flat):
    n_row, n_col, tile = sizes
    group = 2**k
    high = n_col * tile
    wide = n_row * tile
    return pl.pallas_call(
        lambda *refs: schur_kernel(k, sizes, *refs),
        grid=(group,),
        out_shape=[
            jax.ShapeDtypeStruct((high, tile), jnp.float32),
            jax.ShapeDtypeStruct((high, group * wide), jnp.float32),
        ],
        in_specs=[
            pl.BlockSpec(memory_space=pltpu.SMEM),
            pl.BlockSpec((None, high, high), lambda j: (k, 0, 0)),
            pl.BlockSpec((None, high, high), lambda j: (k, 0, 0)),
            pl.BlockSpec((wide, high), lambda j: (j, 0)),
            pl.BlockSpec((high, wide), lambda j: (0, group - 1 + j)),
        ],
        out_specs=[
            pl.BlockSpec((high, tile), lambda j: (0, 0)),
            pl.BlockSpec((high, wide), lambda j: (0, j)),
        ],
        scratch_shapes=[pltpu.VMEM((high, high), jnp.float32)],
        compiler_params=pltpu.CompilerParams(vmem_limit_bytes=40 * 2**20),
        cost_estimate=pl.CostEstimate(
            flops=12 * (2 * group + 1) * high**3,
            bytes_accessed=4 * (3 * group + 2) * high * high,
            transcendentals=0,
        ),
    )(patches, inverses, rows_piv, columns, flat)


def dot(a, b, contract):
    return lax.dot_general(
        a, b, ((contract), ((), ())), precision=HIGHEST, preferred_element_type=jnp.float32
    )


def local(initials, patches, halves):
    n_level = lax.axis_size("level")
    n_row = lax.axis_size("row")
    n_col = lax.axis_size("col")
    levels = n_level.bit_length()
    lvl = lax.axis_index("level")
    row_idx = lax.axis_index("row")
    col_idx = lax.axis_index("col")
    rows_dev = initials.shape[0]
    tile = rows_dev // n_col
    per_level = n_row * n_col
    sizes = (n_level, n_row, n_col, levels, tile)
    pivot_labels = jnp.stack(
        [
            lax.dynamic_slice_in_dim(patches[k], lvl // 2**k * 2**k * per_level, n_col)
            for k in range(levels)
        ]
    )
    flat = initials[:, 0, :]
    inverses, rows_piv, column_rows = gather_and_invert(
        flat, jnp.repeat(pivot_labels, tile, axis=1), sizes
    )
    update = None
    panel_list = []
    for level_k in range(levels):
        group = 2**level_k
        width = group * n_row * tile
        local_level = lvl % group
        panel, schur = panel_and_schur(
            level_k,
            (n_row, n_col, tile),
            patches,
            inverses,
            rows_piv,
            column_rows[level_k],
            flat,
        )
        if level_k > 0:
            child = group // 2
            side = lvl // child % 2
            partner_lvl = lvl + child - 2 * child * side
            partner_update = from_partner(update, "level", level_k - 1)
            hvec = halves[level_k - 1]
            own_rows = lax.dynamic_slice_in_dim(hvec, per_level * lvl + n_col * row_idx, n_col)
            other_rows = lax.dynamic_slice_in_dim(
                hvec, per_level * partner_lvl + n_col * row_idx, n_col
            )
            own_cols = pick_column(
                hvec, lvl // child * per_level * child, child * n_row, n_col, col_idx
            )
            other_cols = pick_column(
                hvec, partner_lvl // child * per_level * child, child * n_row, n_col, col_idx
            )
            schur = schur + place_update(update, own_rows, own_cols, side, tile)
            schur = schur + place_update(partner_update, other_rows, other_cols, side, tile)
            keep_row = ~((local_level == 0) & (row_idx == 0))
            keep_col = jnp.arange(width) >= tile
            schur = jnp.where(keep_row & keep_col[None, :], schur, 0.0)
        update = schur
        panel_list.append(panel)
    return (jnp.stack(panel_list, axis=0), update[:, None, :])


def solution(mesh):
    placed = (P(("level", "row"), "col", None), P(), P())
    return jax.shard_map(
        local,
        mesh=mesh,
        in_specs=placed,
        out_specs=(P(None, ("level", "row"), "col"), P(("level", "row"), "col", None)),
        check_vma=False,
    )
```
